256 devices in a mesh: row: 16 (over x_lo, y, core), col: 16 (over z, x_hi).
Axes of the slice: x: 4 (x_hi: 2, x_lo: 2; x = x_hi * 2 + x_lo), y: 4, z: 8, core: 2. Of those that a mesh axis runs over, the one named last changes fastest.
Arguments:
- row_vectors: float32 [300, 131072], P(None, ('row', 'col')), may hold values from -0.6 to 0.6
- row_accum: float32 [300, 131072], P(None, ('row', 'col')), may hold values from 0.5 to 8
- row_counts: int32 [131072], P(('row', 'col')), may hold values from 1000 to 1999999
- column_vectors: float32 [300, 131072], P(None, ('row', 'col')), may hold values from -0.6 to 0.6
- column_accum: float32 [300, 131072], P(None, ('row', 'col')), may hold values from 0.5 to 8
- column_counts: int32 [131072], P(('row', 'col')), may hold values from 1000 to 1999999
- counts: int32 [4, 8192, 8192], P(None, 'row', 'col'), may hold values from 0 to 2048, as said below
- log_total: float32 [1], replicated, may hold values from 25 to 29
Outputs:
- new_row_vectors: float32 [300, 131072], P(None, ('row', 'col'))
- new_row_accum: float32 [300, 131072], P(None, ('row', 'col'))
- new_column_vectors: float32 [300, 131072], P(None, ('row', 'col'))
- new_column_accum: float32 [300, 131072], P(None, ('row', 'col'))
- losses: float32 [4, 256], P(None, ('row', 'col'))
The draws below stay inside these ranges and needn't reach their ends.
Inputs may be any that keep to these rules, and one draw needn't show every extreme that they name: Roughly a third of the entries are zero; nonzero counts are spread over magnitudes from 1 upward.
All inputs are finite; a program needn't handle non-finite values.
Results may differ from the reference program's by a relative error of at most 0.0003.
Values sent between devices are 32-bit elements; how exact they have to be, the bound alone decides.
A program may use at most 64 MiB of HBM per device.

```python
import math
import jax
import jax.numpy as jnp
import numpy as np
from jax import lax

D = 300
ROW_DEV = 512
STEPS = 4
VOCAB = 131072
ROW_SPAN = 8192
COL_SPAN = 8192
N_ROW = 16
N_COL = 16


def draw_counts(key, part):
    key = jax.random.fold_in(key, 7)
    key_bits, key_vals, key_keep = jax.random.split(key, 3)
    shape = (STEPS, ROW_SPAN, COL_SPAN)
    levels = jax.random.randint(key_bits, shape, 0, 12)
    raw = jax.random.randint(key_vals, shape, 0, 4096)
    values = 1 + raw % jnp.left_shift(jnp.int32(1), levels)
    keep = jax.random.randint(key_keep, shape, 0, 3) > 0
    out = jnp.where(keep, values, 0).astype(jnp.int32)
    return out.at[:, 0, 0].set(2048)


def touch_ends(result, key, smallest, top_value):
    longest = result.shape.index(max(result.shape))
    spots = []
    for shift in (0, 1):
        where = [jax.random.randint(jax.random.fold_in(key, axis), (), 0, length) for axis, length in enumerate(result.shape)]
        where[longest] = (where[longest] + shift) % result.shape[longest]
        spots.append(tuple(where))
    return result.at[spots[0]].set(smallest).at[spots[1]].set(top_value)


def block_levels(stream_key, extent, shards, smallest, high):
    loudness = 1.0
    for dim, blocks in shards:
        steps = jax.random.uniform(jax.random.fold_in(jax.random.fold_in(stream_key, 6), dim), (blocks,), jnp.float32, smallest / len(shards), high / len(shards))
        loudness = loudness * jnp.repeat(jnp.exp(steps), extent[dim] // blocks).reshape((-1,) + (1,) * (len(extent) - 1 - dim))
    return loudness


def bell_draw(stream_key, dims, scale, limit, pieces=(), held_as=jnp.bfloat16):
    array = scale * jax.random.normal(stream_key, dims, jnp.float32)
    if pieces:
        array = array * block_levels(stream_key, dims, pieces, -0.22, 0.18)
    return jnp.clip(array, -limit, limit).astype(held_as)


def setup_inputs(seed: int = 0) -> dict:
    splits = jax.random.split(jax.random.key(seed), 9)
    row_vectors = bell_draw(splits[0], (D, VOCAB), 0.1, 0.6, ((1, 256),), jnp.float32)
    row_accum = jnp.clip(jnp.exp(math.log(8.0) - 2.7725887 * jax.random.uniform(splits[1], (D, VOCAB), jnp.float32) ** block_levels(splits[1], (D, VOCAB), ((1, 256),), -0.2, 0.2)), 0.5, 8.0)
    row_counts = touch_ends(jax.random.randint(splits[2], (VOCAB,), 1000, 2000000), jax.random.fold_in(splits[2], 1), 1000, 1999999).astype(jnp.int32)
    column_vectors = bell_draw(splits[3], (D, VOCAB), 0.1, 0.6, ((1, 256),), jnp.float32)
    column_accum = jnp.clip(jnp.exp(math.log(8.0) - 2.7725887 * jax.random.uniform(splits[4], (D, VOCAB), jnp.float32) ** block_levels(splits[4], (D, VOCAB), ((1, 256),), -0.2, 0.2)), 0.5, 8.0)
    column_counts = touch_ends(jax.random.randint(splits[5], (VOCAB,), 1000, 2000000), jax.random.fold_in(splits[5], 1), 1000, 1999999).astype(jnp.int32)
    counts = draw_counts(jax.random.fold_in(splits[8], 71), 0)
    log_total = jnp.clip(jax.random.uniform(splits[7], (1,), jnp.float32, 25.0, 29.0), 25.0, 29.0)
    return dict(row_vectors=row_vectors, row_accum=row_accum, row_counts=row_counts, column_vectors=column_vectors, column_accum=column_accum, column_counts=column_counts, counts=counts, log_total=log_total)


def prepare_tile(cnt):
    x = cnt.astype(jnp.float32)
    q = jnp.log(jnp.maximum(x, 1.0))
    conf = jnp.where(cnt > 0, 0.1 + 0.25 * jnp.sqrt(x), jnp.zeros_like(x))
    return (q, conf)

def tile_update(wr, ar, rlg, wc, ac, clg, q, conf, logt):
    pmi = q + logt - rlg[:, None] - clg[None, :]
    logits = lax.dot_general(wr, wc, (((0,), (0,)), ((), ())), precision=lax.Precision.HIGHEST, preferred_element_type=jnp.float32)
    err = logits - pmi
    positive = conf > 0
    scaled = jnp.where(positive, conf * err, jax.nn.sigmoid(err))
    loss = jnp.sum(jnp.where(positive, 0.5 * conf * err * err, jax.nn.softplus(err))) / (err.shape[0] * err.shape[1])
    grad_row = lax.dot_general(wc, scaled, (((1,), (1,)), ((), ())), precision=lax.Precision.HIGHEST, preferred_element_type=jnp.float32)
    grad_col = lax.dot_general(wr, scaled, (((1,), (0,)), ((), ())), precision=lax.Precision.HIGHEST, preferred_element_type=jnp.float32)
    ar_new = ar + grad_row * grad_row
    wr_new = wr - 0.05 * grad_row / jnp.sqrt(ar_new)
    ac_new = ac + grad_col * grad_col
    wc_new = wc - 0.05 * grad_col / jnp.sqrt(ac_new)
    return (wr_new, ar_new, wc_new, ac_new, loss)

def reference(row_vectors, row_accum, row_counts, column_vectors, column_accum, column_counts, counts, log_total):
    nrow, ncol, width = (N_ROW, N_COL, ROW_DEV)
    nblk = nrow * ncol
    depth = row_vectors.shape[0]

    def blocks(arr):
        return arr.reshape(depth, nblk, width).transpose(1, 0, 2)

    def unblock(arr):
        return arr.transpose(1, 0, 2).reshape(depth, nblk * width)
    wrb, arb, wcb, acb = (blocks(row_vectors), blocks(row_accum), blocks(column_vectors), blocks(column_accum))
    rlog = jnp.log(row_counts.astype(jnp.float32)).reshape(nblk, width)
    clog = jnp.log(column_counts.astype(jnp.float32)).reshape(nblk, width)
    logt = log_total[0]
    pairs = np.arange(nblk)
    prow, pcol = (pairs // ncol, pairs % ncol)
    loss_rows = []
    for step in range(STEPS):
        brow = jnp.asarray(prow * ncol + (pcol - step) % ncol, dtype=jnp.int32)
        bcol = jnp.asarray((prow - step) % nrow * ncol + pcol, dtype=jnp.int32)
        tiles = counts[step].reshape(nrow, width, ncol, width).transpose(0, 2, 1, 3).reshape(nblk, width, width)

        def one_pair(item):
            wr, ar, rlg, wc, ac, clg, cnt = item
            q, conf = prepare_tile(cnt)
            return tile_update(wr, ar, rlg, wc, ac, clg, q, conf, logt)
        wr_new, ar_new, wc_new, ac_new, loss = lax.map(one_pair, (wrb[brow], arb[brow], rlog[brow], wcb[bcol], acb[bcol], clog[bcol], tiles))
        wrb = wrb.at[brow].set(wr_new)
        arb = arb.at[brow].set(ar_new)
        wcb = wcb.at[bcol].set(wc_new)
        acb = acb.at[bcol].set(ac_new)
        loss_rows.append(jnp.zeros((nblk,), jnp.float32).at[bcol].set(loss))
    return (unblock(wrb), unblock(arb), unblock(wcb), unblock(acb), jnp.stack(loss_rows))
```

```python
import functools

import jax
import jax.numpy as jnp
from jax import lax
from jax.experimental import pallas as pl
from jax.experimental.pallas import tpu as pltpu
from jax.sharding import PartitionSpec as P

MESH = pl.DeviceIdType.MESH
F32 = jnp.float32
BF16 = jnp.bfloat16
CHUNK = 128
ROW_BLOCK = 128


def halves(x):
    hi = x.astype(BF16)
    return hi, (x - hi.astype(F32)).astype(BF16)


def product(a_hi, a_lo, b_hi, b_lo, dims):
    def dot(a, b):
        return lax.dot_general(a, b, (dims, ((), ())), preferred_element_type=F32)

    return dot(a_hi, b_hi) + (dot(a_hi, b_lo) + dot(a_lo, b_hi))


def kernel(
    depth,
    rows,
    cols,
    row_vec,
    row_acc,
    row_cnt,
    col_vec,
    col_acc,
    col_cnt,
    counts,
    log_total,
    out_row_vec,
    out_row_acc,
    out_col_vec,
    out_col_acc,
    out_losses,
    tiles,
    r_vec,
    r_acc,
    c_vec,
    c_acc,
    visitor_in,
    grad_out,
    grad_in,
    base,
    conf,
    r_col,
    c_col,
    y_hi,
    y_lo,
    yt_hi,
    yt_lo,
    x_hi,
    x_lo,
    e_hi,
    e_lo,
    host_grad,
    local_sem,
    tile_send,
    tile_recv,
    out_send,
    out_recv,
    back_send,
    back_recv,
):
    nchunk, padded, width = r_vec.shape
    words = row_vec.shape[1]
    kpad = x_hi.shape[1]
    r, c = lax.axis_index("row"), lax.axis_index("col")

    def at(dr, dc):
        return (lax.rem(r + dr + rows, rows), lax.rem(c + dc + cols, cols))

    def lanes(k):
        return pl.ds(pl.multiple_of(k * width, width), width)

    target = (at(-1, 1), at(2, -2), at(-3, 3))
    source = (at(1, -1), at(-2, 2), at(3, -3))
    tile_target = (at(-1, 0), at(0, -2), at(-3, 0))
    tile_source = (at(1, 0), at(0, 2), at(3, 0))

    barrier = pltpu.get_barrier_semaphore()
    for device in target + source + tile_source:
        pl.semaphore_signal(barrier, inc=1, device_id=device, device_id_type=MESH)

    first_tile = pltpu.make_async_copy(counts.at[0], tiles.at[0], local_sem)
    first_tile.start()

    def tile_copy(i):
        return pltpu.make_async_remote_copy(
            src_ref=counts.at[i + 1],
            dst_ref=tiles.at[i + 1],
            send_sem=tile_send.at[i],
            recv_sem=tile_recv.at[i],
            device_id=tile_target[i],
            device_id_type=MESH,
        )

    def out_copy(i, k):
        return pltpu.make_async_remote_copy(
            src_ref=(c_vec if i == 1 else r_vec).at[k],
            dst_ref=visitor_in.at[i, k],
            send_sem=out_send.at[i, k],
            recv_sem=out_recv.at[i, k],
            device_id=target[i],
            device_id_type=MESH,
        )

    def back_copy(i, k):
        return pltpu.make_async_remote_copy(
            src_ref=grad_out.at[i, k],
            dst_ref=grad_in.at[i, k],
            send_sem=back_send.at[i, k],
            recv_sem=back_recv.at[i, k],
            device_id=source[i],
            device_id_type=MESH,
        )

    def each_chunk(body):
        def step(k, carry):
            body(k)
            return carry

        lax.fori_loop(0, nchunk, step, 0)

    logt = log_total[0]
    real = lax.broadcasted_iota(jnp.int32, (padded, width), 0) < depth

    def fill(vec, acc, vec_in, acc_in, cnt, column):
        logs = jnp.log(cnt[...].astype(F32))
        column[...] = jnp.transpose(jnp.broadcast_to(logs, (128, words)))
        for k in range(nchunk):
            part = slice(k * width, (k + 1) * width)
            vec[k, 0:depth, :] = vec_in[:, part]
            vec[k, depth : depth + 1, :] = logs[:, part]
            vec[k, depth + 1 : padded, :] = jnp.zeros((padded - depth - 1, width), F32)
            acc[k, 0:depth, :] = acc_in[:, part]
            acc[k, depth:padded, :] = jnp.ones((padded - depth, width), F32)

    def host_chunk(vec, k):
        x = jnp.where(real, vec[k], 0.0)
        y_hi[:, lanes(k)], y_lo[:, lanes(k)] = halves(x)
        xt = jnp.transpose(jnp.concatenate([x, jnp.zeros((kpad - padded, width), F32)], axis=0))
        yt_hi[lanes(k), :], yt_lo[lanes(k), :] = halves(xt)

    def prepare(i, k, column, turned):
        if turned:
            x = jnp.transpose(tiles[i, lanes(k), :].astype(F32))
        else:
            x = tiles[i, :, lanes(k)].astype(F32)
        q = jnp.log(jnp.maximum(x, 1.0))
        base[k] = (q + logt) - column[:, 0:1]
        conf[k] = jnp.where(x > 0, 0.1 + 0.25 * jnp.sqrt(x), 0.0)

    def visit(x, k):
        words_log = x[depth : depth + 1, :]
        x_hi[k, 0:padded, :], x_lo[k, 0:padded, :] = halves(jnp.where(real, x, 0.0))
        loss = jnp.zeros((8, width), F32)
        for start in range(0, words, ROW_BLOCK):
            part = slice(start, start + ROW_BLOCK)
            logits = product(
                yt_hi[part, :], yt_lo[part, :], x_hi[k], x_lo[k], ((1,), (0,))
            )
            weight = conf[k, part, :]
            err = logits - (base[k, part, :] - words_log)
            small = jnp.exp(-jnp.abs(err))
            positive = weight > 0
            scaled = jnp.where(
                positive, weight * err, jnp.where(err >= 0, 1.0, small) / (1.0 + small)
            )
            cell = jnp.where(
                positive, 0.5 * scaled * err, jnp.maximum(err, 0.0) + jnp.log1p(small)
            )
            loss = loss + jnp.sum(cell.reshape(ROW_BLOCK // 8, 8, width), axis=0)
            e_hi[k, part, :], e_lo[k, part, :] = halves(scaled)
        grad = product(y_hi[...], y_lo[...], e_hi[k], e_lo[k], ((1,), (0,)))
        return grad, jnp.sum(loss, axis=0, keepdims=True)

    def host_add(k):
        host_grad[...] += product(
            x_hi[k, 0:padded, :], x_lo[k, 0:padded, :], e_hi[k], e_lo[k], ((1,), (1,))
        )

    def update(vec, acc, k, grad):
        total = acc[k] + grad * grad
        acc[k] = total
        vec[k] = vec[k] - 0.05 * (grad * lax.rsqrt(total))

    def store_loss(s, row):
        out_losses[s : s + 1, 0:1] = jnp.sum(row, axis=1, keepdims=True) * (1.0 / (words * words))

    fill(c_vec, c_acc, col_vec, col_acc, col_cnt, c_col)
    fill(r_vec, r_acc, row_vec, row_acc, row_cnt, r_col)
    x_hi[...] = jnp.zeros_like(x_hi)
    x_lo[...] = jnp.zeros_like(x_lo)
    each_chunk(lambda k: host_chunk(c_vec, k))
    host_grad[...] = jnp.zeros_like(host_grad)

    pl.semaphore_wait(barrier, 9)
    tile_copy(0).start()
    tile_copy(1).start()
    first_tile.wait()

    def step0(k, total):
        prepare(0, k, c_col, True)
        grad, loss = visit(r_vec[k], k)
        update(r_vec, r_acc, k, grad)
        out_copy(0, k).start()
        host_add(k)
        return total + loss

    zero = jnp.zeros((1, width), F32)
    store_loss(0, lax.fori_loop(0, nchunk, step0, zero))

    def c_update(k):
        update(c_vec, c_acc, k, host_grad[:, lanes(k)])
        host_chunk(c_vec, k)

    each_chunk(c_update)
    host_grad[...] = jnp.zeros_like(host_grad)

    tile_copy(0).wait()
    each_chunk(lambda k: prepare(1, k, c_col, True))

    def visited(i, k, total):
        out_copy(i, k).wait_recv()
        grad, loss = visit(visitor_in[i, k], k)
        grad_out[i, k] = grad
        if i == 1:
            grad_out[i, k, depth + 1 : depth + 2, :] = loss
        back_copy(i, k).start()
        host_add(k)
        return total + loss

    store_loss(1, lax.fori_loop(0, nchunk, lambda k, t: visited(0, k, t), zero))

    def c_sent(k):
        update(c_vec, c_acc, k, host_grad[:, lanes(k)])
        out_copy(1, k).start()

    each_chunk(c_sent)
    tile_copy(2).start()
    host_grad[...] = jnp.zeros_like(host_grad)

    tile_copy(1).wait()
    each_chunk(lambda k: prepare(2, k, r_col, False))

    def r_back(k):
        out_copy(0, k).wait_send()
        back_copy(0, k).wait_recv()
        update(r_vec, r_acc, k, grad_in[0, k])
        host_chunk(r_vec, k)

    each_chunk(r_back)
    lax.fori_loop(0, nchunk, lambda k, t: visited(1, k, t), zero)

    def r_sent(k):
        update(r_vec, r_acc, k, host_grad[:, lanes(k)])
        out_copy(2, k).start()

    each_chunk(r_sent)
    host_grad[...] = jnp.zeros_like(host_grad)

    tile_copy(2).wait()
    each_chunk(lambda k: prepare(3, k, c_col, True))

    def c_back(k, total):
        out_copy(1, k).wait_send()
        back_copy(1, k).wait_recv()
        update(c_vec, c_acc, k, grad_in[1, k])
        host_chunk(c_vec, k)
        return total + grad_in[1, k, depth + 1 : depth + 2, :]

    store_loss(2, lax.fori_loop(0, nchunk, c_back, zero))
    store_loss(3, lax.fori_loop(0, nchunk, lambda k, t: visited(2, k, t), zero))

    def c_last(k):
        update(c_vec, c_acc, k, host_grad[:, lanes(k)])
        out_col_vec[:, lanes(k)] = c_vec[k, 0:depth, :]
        out_col_acc[:, lanes(k)] = c_acc[k, 0:depth, :]

    each_chunk(c_last)

    def r_last(k):
        out_copy(2, k).wait_send()
        back_copy(2, k).wait_recv()
        update(r_vec, r_acc, k, grad_in[2, k])
        out_row_vec[:, lanes(k)] = r_vec[k, 0:depth, :]
        out_row_acc[:, lanes(k)] = r_acc[k, 0:depth, :]

    each_chunk(r_last)

    def sent(k):
        for i in range(3):
            back_copy(i, k).wait_send()

    each_chunk(sent)


def local(mesh, row_vec, row_acc, row_cnt, col_vec, col_acc, col_cnt, counts, log_total):
    depth, words = row_vec.shape
    nsteps = counts.shape[0]
    padded = -(-depth // 16) * 16
    kpad = -(-depth // 128) * 128
    nchunk = words // CHUNK
    chunks = (nchunk, padded, CHUNK)
    block = jax.ShapeDtypeStruct((depth, words), F32)
    vmem = pl.BlockSpec(memory_space=pltpu.VMEM)
    dma = pltpu.SemaphoreType.DMA
    return pl.pallas_call(
        functools.partial(kernel, depth, mesh.shape["row"], mesh.shape["col"]),
        out_shape=(block,) * 4 + (jax.ShapeDtypeStruct((nsteps, 1), F32),),
        in_specs=[vmem] * 6
        + [pl.BlockSpec(memory_space=pl.ANY), pl.BlockSpec(memory_space=pltpu.SMEM)],
        out_specs=(vmem,) * 5,
        scratch_shapes=[
            pltpu.VMEM((nsteps, words, words), jnp.int32),
            pltpu.VMEM(chunks, F32),
            pltpu.VMEM(chunks, F32),
            pltpu.VMEM(chunks, F32),
            pltpu.VMEM(chunks, F32),
            pltpu.VMEM((3,) + chunks, F32),
            pltpu.VMEM((3,) + chunks, F32),
            pltpu.VMEM((3,) + chunks, F32),
            pltpu.VMEM((nchunk, words, CHUNK), F32),
            pltpu.VMEM((nchunk, words, CHUNK), F32),
            pltpu.VMEM((words, 128), F32),
            pltpu.VMEM((words, 128), F32),
            pltpu.VMEM((padded, words), BF16),
            pltpu.VMEM((padded, words), BF16),
            pltpu.VMEM((words, kpad), BF16),
            pltpu.VMEM((words, kpad), BF16),
            pltpu.VMEM((nchunk, kpad, CHUNK), BF16),
            pltpu.VMEM((nchunk, kpad, CHUNK), BF16),
            pltpu.VMEM((nchunk, words, CHUNK), BF16),
            pltpu.VMEM((nchunk, words, CHUNK), BF16),
            pltpu.VMEM((padded, words), F32),
            dma(()),
            dma((3,)),
            dma((3,)),
            dma((3, nchunk)),
            dma((3, nchunk)),
            dma((3, nchunk)),
            dma((3, nchunk)),
        ],
        compiler_params=pltpu.CompilerParams(
            collective_id=0, has_side_effects=True, vmem_limit_bytes=48 * 1024 * 1024
        ),
        name="swivel",
    )(
        row_vec,
        row_acc,
        row_cnt.reshape(1, words),
        col_vec,
        col_acc,
        col_cnt.reshape(1, words),
        counts,
        log_total,
    )


def solution(mesh):
    both = P(None, ("row", "col"))
    one = P(("row", "col"))
    return jax.shard_map(
        functools.partial(local, mesh),
        mesh=mesh,
        in_specs=(both, both, one, both, both, one, P(None, "row", "col"), P()),
        out_specs=(both,) * 5,
        check_vma=False,
    )
```

```python
import functools

import jax
import jax.numpy as jnp
from jax import lax
from jax.experimental import pallas as pl
from jax.experimental.pallas import tpu as pltpu
from jax.sharding import PartitionSpec as P

MESH = pl.DeviceIdType.MESH
F32 = jnp.float32
BF16 = jnp.bfloat16
CHUNK = 128
ROW_BLOCK = 128


def halves(x):
    hi = x.astype(BF16)
    return hi, (x - hi.astype(F32)).astype(BF16)


def product(a_hi, a_lo, b_hi, b_lo, dims):
    def dot(a, b):
        return lax.dot_general(a, b, (dims, ((), ())), preferred_element_type=F32)

    return dot(a_hi, b_hi) + (dot(a_hi, b_lo) + dot(a_lo, b_hi))


def kernel(
    depth,
    rows,
    cols,
    row_vec_hbm,
    row_acc_hbm,
    row_cnt_hbm,
    col_vec_hbm,
    col_acc_hbm,
    col_cnt_hbm,
    counts,
    log_total,
    out_row_vec,
    out_row_acc,
    out_col_vec,
    out_col_acc,
    out_losses,
    row_vec,
    row_acc,
    row_cnt,
    col_vec,
    col_acc,
    col_cnt,
    tiles,
    r_vec,
    r_acc,
    c_vec,
    c_acc,
    visitor_in,
    grad_out,
    grad_in,
    base,
    conf,
    r_col,
    c_col,
    y_hi,
    y_lo,
    yt_hi,
    yt_lo,
    x_hi,
    x_lo,
    e_hi,
    e_lo,
    host_grad,
    loss_sum,
    local_sem,
    tile_send,
    tile_recv,
    out_send,
    out_recv,
    back_send,
    back_recv,
):
    nchunk, padded, width = r_vec.shape
    words = row_vec.shape[1]
    kpad = x_hi.shape[0]
    r, c = lax.axis_index("row"), lax.axis_index("col")

    def at(dr, dc):
        return (lax.rem(r + dr + rows, rows), lax.rem(c + dc + cols, cols))

    def lanes(k, size=width):
        return pl.ds(pl.multiple_of(k * size, size), size)

    target = (at(-1, 1), at(2, -2), at(-3, 3))
    source = (at(1, -1), at(-2, 2), at(3, -3))
    tile_target = (at(-1, 0), at(0, -2), at(-3, 0))
    tile_source = (at(1, 0), at(0, 2), at(3, 0))

    barrier = pltpu.get_barrier_semaphore()
    for device in target + source + tile_source:
        pl.semaphore_signal(barrier, inc=1, device_id=device, device_id_type=MESH)

    loads = [
        pltpu.make_async_copy(src, dst, local_sem.at[i])
        for i, (src, dst) in enumerate(
            (
                (col_cnt_hbm, col_cnt),
                (col_vec_hbm, col_vec),
                (counts.at[0], tiles.at[0]),
                (row_cnt_hbm, row_cnt),
                (row_vec_hbm, row_vec),
                (row_acc_hbm, row_acc),
                (col_acc_hbm, col_acc),
            )
        )
    ]
    for load in loads:
        load.start()

    def tile_copy(i, k):
        rows_k = pl.ds(pl.multiple_of(k * width, width), width)
        return pltpu.make_async_remote_copy(
            src_ref=counts.at[i + 1, rows_k],
            dst_ref=tiles.at[i + 1, rows_k],
            send_sem=tile_send.at[i, k],
            recv_sem=tile_recv.at[i, k],
            device_id=tile_target[i],
            device_id_type=MESH,
        )

    def out_copy(i, k):
        return pltpu.make_async_remote_copy(
            src_ref=(c_vec if i == 1 else r_vec).at[k],
            dst_ref=visitor_in.at[i, k],
            send_sem=out_send.at[i, k],
            recv_sem=out_recv.at[i, k],
            device_id=target[i],
            device_id_type=MESH,
        )

    def back_copy(i, k):
        return pltpu.make_async_remote_copy(
            src_ref=grad_out.at[i, k],
            dst_ref=grad_in.at[i, k],
            send_sem=back_send.at[i, k],
            recv_sem=back_recv.at[i, k],
            device_id=source[i],
            device_id_type=MESH,
        )

    def each_chunk(body):
        def step(k, carry):
            body(k)
            return carry

        lax.fori_loop(0, nchunk, step, 0)

    logt = log_total[0]

    def real(x):
        return jnp.where(lax.broadcasted_iota(jnp.int32, x.shape, 0) < depth, x, 0.0)

    def fill(vec, acc, vec_in, acc_in, cnt, column):
        logs = jnp.log(cnt[...].astype(F32))
        column[...] = jnp.transpose(jnp.broadcast_to(logs, (128, words)))
        for k in range(nchunk):
            part = slice(k * width, (k + 1) * width)
            vec[k, 0:depth, :] = vec_in[:, part]
            vec[k, depth : depth + 1, :] = logs[:, part]
            vec[k, depth + 1 : padded, :] = jnp.zeros((padded - depth - 1, width), F32)
            acc[k, 0:depth, :] = acc_in[:, part]
            acc[k, depth:padded, :] = jnp.ones((padded - depth, width), F32)

    def host_chunk(vec, k):
        x = real(vec[k])
        y_hi[:, lanes(k)], y_lo[:, lanes(k)] = halves(x)
        xt = jnp.transpose(jnp.concatenate([x, jnp.zeros((kpad - padded, width), F32)], axis=0))
        yt_hi[lanes(k), :], yt_lo[lanes(k), :] = halves(xt)

    def prepare(i, k, column, turned):
        if turned:
            x = jnp.transpose(tiles[i, lanes(k), :].astype(F32))
        else:
            x = tiles[i, :, lanes(k)].astype(F32)
        q = jnp.log(jnp.maximum(x, 1.0))
        base[:, lanes(k)] = (q + logt) - column[:, 0:1]
        conf[:, lanes(k)] = jnp.where(x > 0, 0.1 + 0.25 * jnp.sqrt(x), 0.0)

    def visit(s, x, where):
        size = x.shape[1]
        words_log = x[depth : depth + 1, :]
        x_hi[0:padded, where], x_lo[0:padded, where] = halves(real(x))
        loss = jnp.zeros((8, size), F32)
        for start in range(0, words, ROW_BLOCK):
            part = slice(start, start + ROW_BLOCK)
            logits = product(
                yt_hi[part, :], yt_lo[part, :], x_hi[:, where], x_lo[:, where], ((1,), (0,))
            )
            weight = conf[part, where]
            err = logits - (base[part, where] - words_log)
            small = jnp.exp(-jnp.abs(err))
            positive = weight > 0
            scaled = jnp.where(
                positive, weight * err, jnp.where(err >= 0, 1.0, small) / (1.0 + small)
            )
            cell = jnp.where(
                positive, 0.5 * scaled * err, jnp.maximum(err, 0.0) + jnp.log1p(small)
            )
            loss = loss + jnp.sum(cell.reshape(ROW_BLOCK // 8, 8, size), axis=0)
            e_hi[part, where], e_lo[part, where] = halves(scaled)
        grad = product(y_hi[...], y_lo[...], e_hi[:, where], e_lo[:, where], ((1,), (0,)))
        for start in range(0, size, width):
            loss_sum[s : s + 1, :] += jnp.sum(loss[:, start : start + width], axis=0, keepdims=True)
        return grad

    def host_add(pair):
        where = lanes(pair, 2 * width)
        host_grad[...] += product(
            x_hi[0:padded, where], x_lo[0:padded, where], e_hi[:, where], e_lo[:, where], ((1,), (1,))
        )

    def host_add_odd(k):
        @pl.when(lax.rem(k, 2) == 1)
        def _():
            host_add(lax.div(k, 2))

    def update(vec, acc, k, grad):
        total = acc[k] + grad * grad
        acc[k] = total
        vec[k] = vec[k] - 0.05 * (grad * lax.rsqrt(total))

    x_hi[...] = jnp.zeros_like(x_hi)
    x_lo[...] = jnp.zeros_like(x_lo)
    loss_sum[...] = jnp.zeros_like(loss_sum)
    host_grad[...] = jnp.zeros_like(host_grad)
    pl.semaphore_wait(barrier, 9)
    each_chunk(lambda k: tile_copy(0, k).start())
    each_chunk(lambda k: tile_copy(1, k).start())
    for load in loads:
        load.wait()
    fill(c_vec, c_acc, col_vec, col_acc, col_cnt, c_col)
    fill(r_vec, r_acc, row_vec, row_acc, row_cnt, r_col)
    each_chunk(lambda k: host_chunk(c_vec, k))

    def step0(k):
        prepare(0, k, c_col, True)
        grad = visit(0, r_vec[k], lanes(k))
        update(r_vec, r_acc, k, grad)
        out_copy(0, k).start()
        host_add_odd(k)

    each_chunk(step0)

    def c_update(k):
        update(c_vec, c_acc, k, host_grad[:, lanes(k)])
        host_chunk(c_vec, k)

    each_chunk(c_update)
    host_grad[...] = jnp.zeros_like(host_grad)

    far = lax.rem(r, 8) < 3

    @pl.when(jnp.logical_not(far))
    def _():
        each_chunk(lambda k: tile_copy(2, k).start())

    def visited(i, k):
        tile_copy(i, k).wait_recv()
        prepare(i + 1, k, c_col, True)
        out_copy(i, k).wait_recv()
        grad_out[i, k] = visit(i + 1, visitor_in[i, k], lanes(k))
        back_copy(i, k).start()
        host_add_odd(k)

    each_chunk(lambda k: visited(0, k))

    def c_sent(k):
        update(c_vec, c_acc, k, host_grad[:, lanes(k)])
        out_copy(1, k).start()

    each_chunk(c_sent)

    @pl.when(far)
    def _():
        each_chunk(lambda k: tile_copy(2, k).start())

    host_grad[...] = jnp.zeros_like(host_grad)

    each_chunk(lambda k: tile_copy(1, k).wait_recv())
    each_chunk(lambda k: prepare(2, k, r_col, False))

    def r_back(k):
        out_copy(0, k).wait_send()
        back_copy(0, k).wait_recv()
        update(r_vec, r_acc, k, grad_in[0, k])
        host_chunk(r_vec, k)

    each_chunk(r_back)

    def visited_pair(pair, carry):
        ks = [2 * pair, 2 * pair + 1]
        for k in ks:
            out_copy(1, k).wait_recv()
        x = jnp.concatenate([visitor_in[1, k] for k in ks], axis=1)
        grad = visit(2, x, lanes(pair, 2 * width))
        for j, k in enumerate(ks):
            grad_out[1, k] = grad[:, j * width : (j + 1) * width]
        grad_out[1, ks[1], depth + 1 : depth + 2, :] = loss_sum[2:3, :]
        for k in ks:
            back_copy(1, k).start()
        host_add(pair)
        return carry

    lax.fori_loop(0, nchunk // 2, visited_pair, 0)

    def r_sent(k):
        update(r_vec, r_acc, k, host_grad[:, lanes(k)])
        out_copy(2, k).start()

    each_chunk(r_sent)
    host_grad[...] = jnp.zeros_like(host_grad)

    def c_back(k):
        out_copy(1, k).wait_send()
        back_copy(1, k).wait_recv()
        update(c_vec, c_acc, k, grad_in[1, k])
        host_chunk(c_vec, k)

    each_chunk(c_back)
    each_chunk(lambda k: visited(2, k))

    def c_last(k):
        update(c_vec, c_acc, k, host_grad[:, lanes(k)])
        out_col_vec[:, lanes(k)] = c_vec[k, 0:depth, :]
        out_col_acc[:, lanes(k)] = c_acc[k, 0:depth, :]

    each_chunk(c_last)
    loss_sum[2:3, :] = grad_in[1, nchunk - 1, depth + 1 : depth + 2, :]
    for s in range(loss_sum.shape[0]):
        total = jnp.sum(loss_sum[s : s + 1, :], axis=1, keepdims=True)
        out_losses[0:1, s : s + 1] = total * (1.0 / (words * words))

    def r_last(k):
        out_copy(2, k).wait_send()
        back_copy(2, k).wait_recv()
        update(r_vec, r_acc, k, grad_in[2, k])
        out_row_vec[:, lanes(k)] = r_vec[k, 0:depth, :]
        out_row_acc[:, lanes(k)] = r_acc[k, 0:depth, :]

    each_chunk(r_last)

    def sent(k):
        for i in range(3):
            back_copy(i, k).wait_send()
            tile_copy(i, k).wait_send()

    each_chunk(sent)


def deliver(*refs):
    count = len(refs) // 2
    for src, dst in zip(refs[:count], refs[count:]):
        dst[...] = src[...]


def local(mesh, row_vec, row_acc, row_cnt, col_vec, col_acc, col_cnt, counts, log_total):
    depth, words = row_vec.shape
    nsteps = counts.shape[0]
    padded = -(-depth // 16) * 16
    kpad = -(-depth // 128) * 128
    nchunk = words // CHUNK
    chunks = (nchunk, padded, CHUNK)
    block = jax.ShapeDtypeStruct((depth, words), F32)
    vmem = pl.BlockSpec(memory_space=pltpu.VMEM)
    dma = pltpu.SemaphoreType.DMA
    hbm = pl.BlockSpec(memory_space=pltpu.HBM)
    results = (block,) * 4 + (jax.ShapeDtypeStruct((1, nsteps), F32),)
    trained = pl.pallas_call(
        functools.partial(kernel, depth, mesh.shape["row"], mesh.shape["col"]),
        out_shape=results,
        in_specs=[hbm] * 7 + [pl.BlockSpec(memory_space=pltpu.SMEM)],
        out_specs=(vmem,) * 5,
        scratch_shapes=[
            pltpu.VMEM((depth, words), F32),
            pltpu.VMEM((depth, words), F32),
            pltpu.VMEM((1, words), jnp.int32),
            pltpu.VMEM((depth, words), F32),
            pltpu.VMEM((depth, words), F32),
            pltpu.VMEM((1, words), jnp.int32),
            pltpu.VMEM((nsteps, words, words), jnp.int32),
            pltpu.VMEM(chunks, F32),
            pltpu.VMEM(chunks, F32),
            pltpu.VMEM(chunks, F32),
            pltpu.VMEM(chunks, F32),
            pltpu.VMEM((3,) + chunks, F32),
            pltpu.VMEM((3,) + chunks, F32),
            pltpu.VMEM((3,) + chunks, F32),
            pltpu.VMEM((words, words), F32),
            pltpu.VMEM((words, words), F32),
            pltpu.VMEM((words, 128), F32),
            pltpu.VMEM((words, 128), F32),
            pltpu.VMEM((padded, words), BF16),
            pltpu.VMEM((padded, words), BF16),
            pltpu.VMEM((words, kpad), BF16),
            pltpu.VMEM((words, kpad), BF16),
            pltpu.VMEM((kpad, words), BF16),
            pltpu.VMEM((kpad, words), BF16),
            pltpu.VMEM((words, words), BF16),
            pltpu.VMEM((words, words), BF16),
            pltpu.VMEM((padded, words), F32),
            pltpu.VMEM((nsteps, CHUNK), F32),
            dma((7,)),
            dma((3, nchunk)),
            dma((3, nchunk)),
            dma((3, nchunk)),
            dma((3, nchunk)),
            dma((3, nchunk)),
            dma((3, nchunk)),
        ],
        compiler_params=pltpu.CompilerParams(
            collective_id=0, has_side_effects=True, vmem_limit_bytes=62 * 1024 * 1024
        ),
        name="swivel",
    )(
        row_vec,
        row_acc,
        row_cnt.reshape(1, words),
        col_vec,
        col_acc,
        col_cnt.reshape(1, words),
        counts,
        log_total,
    )
    *arrays, losses = pl.pallas_call(
        deliver,
        out_shape=results,
        in_specs=[vmem] * 5,
        out_specs=(vmem,) * 5,
        name="deliver",
    )(*trained)
    return (*arrays, losses.T)


def solution(mesh):
    both = P(None, ("row", "col"))
    one = P(("row", "col"))
    return jax.shard_map(
        functools.partial(local, mesh),
        mesh=mesh,
        in_specs=(both, both, one, both, both, one, P(None, "row", "col"), P()),
        out_specs=(both,) * 5,
        check_vma=False,
    )
```

```python
import functools

import jax
import jax.numpy as jnp
from jax import lax
from jax.experimental import pallas as pl
from jax.experimental.pallas import tpu as pltpu
from jax.sharding import PartitionSpec as P

MESH = pl.DeviceIdType.MESH
F32 = jnp.float32
BF16 = jnp.bfloat16
CHUNK = 128
ROW_BLOCK = 128


def halves(x):
    hi = x.astype(BF16)
    return hi, (x - hi.astype(F32)).astype(BF16)


def product(a_hi, a_lo, b_hi, b_lo, dims):
    def dot(a, b):
        return lax.dot_general(a, b, (dims, ((), ())), preferred_element_type=F32)

    return dot(a_hi, b_hi) + (dot(a_hi, b_lo) + dot(a_lo, b_hi))


def kernel(
    depth,
    rows,
    cols,
    row_vec_hbm,
    row_acc_hbm,
    row_cnt_hbm,
    col_vec_hbm,
    col_acc_hbm,
    col_cnt_hbm,
    counts,
    log_total,
    out_row_vec,
    out_row_acc,
    out_col_vec,
    out_col_acc,
    out_losses,
    out_stage,
    row_vec,
    row_acc,
    row_cnt,
    col_vec,
    col_acc,
    col_cnt,
    tiles,
    r_vec,
    r_acc,
    c_vec,
    c_acc,
    visitor_in,
    grad_out,
    grad_in,
    base,
    conf,
    r_col,
    c_col,
    y_hi,
    y_lo,
    yt_hi,
    yt_lo,
    x_hi,
    x_lo,
    e_hi,
    e_lo,
    host_grad,
    loss_sum,
    local_sem,
    tile_send,
    tile_recv,
    out_send,
    out_recv,
    back_send,
    back_recv,
    store_sem,
):
    nchunk, padded, width = r_vec.shape
    words = row_vec.shape[1]
    kpad = x_hi.shape[0]
    r, c = lax.axis_index("row"), lax.axis_index("col")

    def at(dr, dc):
        return (lax.rem(r + dr + rows, rows), lax.rem(c + dc + cols, cols))

    def lanes(k, size=width):
        return pl.ds(pl.multiple_of(k * size, size), size)

    target = (at(-1, 1), at(2, -2), at(-3, 3))
    source = (at(1, -1), at(-2, 2), at(3, -3))
    tile_target = (at(-1, 0), at(0, -2), at(-3, 0))
    tile_source = (at(1, 0), at(0, 2), at(3, 0))

    barrier = pltpu.get_barrier_semaphore()
    for device in target + source + tile_source:
        pl.semaphore_signal(barrier, inc=1, device_id=device, device_id_type=MESH)

    loads = [
        pltpu.make_async_copy(src, dst, local_sem.at[i])
        for i, (src, dst) in enumerate(
            (
                (col_cnt_hbm, col_cnt),
                (col_vec_hbm, col_vec),
                (counts.at[0], tiles.at[0]),
                (row_cnt_hbm, row_cnt),
                (row_vec_hbm, row_vec),
                (row_acc_hbm, row_acc),
                (col_acc_hbm, col_acc),
            )
        )
    ]
    for load in loads:
        load.start()

    def tile_copy(i, k):
        rows_k = pl.ds(pl.multiple_of(k * width, width), width)
        return pltpu.make_async_remote_copy(
            src_ref=counts.at[i + 1, rows_k],
            dst_ref=tiles.at[i + 1, rows_k],
            send_sem=tile_send.at[i, k],
            recv_sem=tile_recv.at[i, k],
            device_id=tile_target[i],
            device_id_type=MESH,
        )

    def out_copy(i, k):
        return pltpu.make_async_remote_copy(
            src_ref=(c_vec if i == 1 else r_vec).at[k],
            dst_ref=visitor_in.at[i, k],
            send_sem=out_send.at[i, k],
            recv_sem=out_recv.at[i, k],
            device_id=target[i],
            device_id_type=MESH,
        )

    def back_copy(i, k):
        return pltpu.make_async_remote_copy(
            src_ref=grad_out.at[i, k],
            dst_ref=grad_in.at[i, k],
            send_sem=back_send.at[i, k],
            recv_sem=back_recv.at[i, k],
            device_id=source[i],
            device_id_type=MESH,
        )

    def each_chunk(body):
        def step(k, carry):
            body(k)
            return carry

        lax.fori_loop(0, nchunk, step, 0)

    logt = log_total[0]

    def real(x):
        return jnp.where(lax.broadcasted_iota(jnp.int32, x.shape, 0) < depth, x, 0.0)

    def fill(vec, vec_in, cnt):
        logs = jnp.log(cnt[...].astype(F32))
        for k in range(nchunk):
            part = slice(k * width, (k + 1) * width)
            vec[k, 0:depth, :] = vec_in[:, part]
            vec[k, depth : depth + 1, :] = logs[:, part]
            vec[k, depth + 1 : padded, :] = jnp.zeros((padded - depth - 1, width), F32)
        return logs

    def fill_acc(acc, acc_in):
        for k in range(nchunk):
            acc[k, 0:depth, :] = acc_in[:, k * width : (k + 1) * width]
            acc[k, depth:padded, :] = jnp.ones((padded - depth, width), F32)

    def turned(logs):
        return jnp.transpose(jnp.broadcast_to(logs, (128, words)))

    def host_chunk(vec, k):
        x = real(vec[k])
        y_hi[:, lanes(k)], y_lo[:, lanes(k)] = halves(x)
        xt = jnp.transpose(jnp.concatenate([x, jnp.zeros((kpad - padded, width), F32)], axis=0))
        yt_hi[lanes(k), :], yt_lo[lanes(k), :] = halves(xt)

    def prepare(i, k, column, turned):
        if turned:
            x = jnp.transpose(tiles[i, lanes(k), :].astype(F32))
        else:
            x = tiles[i, :, lanes(k)].astype(F32)
        q = jnp.log(jnp.maximum(x, 1.0))
        base[:, lanes(k)] = (q + logt) - column[:, 0:1]
        conf[:, lanes(k)] = jnp.where(x > 0, 0.1 + 0.25 * jnp.sqrt(x), 0.0)

    def visit(s, x, where):
        size = x.shape[1]
        words_log = x[depth : depth + 1, :]
        x_hi[0:padded, where], x_lo[0:padded, where] = halves(real(x))
        loss = jnp.zeros((8, size), F32)
        for start in range(0, words, ROW_BLOCK):
            part = slice(start, start + ROW_BLOCK)
            logits = product(
                yt_hi[part, :], yt_lo[part, :], x_hi[:, where], x_lo[:, where], ((1,), (0,))
            )
            weight = conf[part, where]
            err = logits - (base[part, where] - words_log)
            small = jnp.exp(-jnp.abs(err))
            positive = weight > 0
            scaled = jnp.where(
                positive, weight * err, jnp.where(err >= 0, 1.0, small) / (1.0 + small)
            )
            cell = jnp.where(
                positive, 0.5 * scaled * err, jnp.maximum(err, 0.0) + jnp.log1p(small)
            )
            loss = loss + jnp.sum(cell.reshape(ROW_BLOCK // 8, 8, size), axis=0)
            e_hi[part, where], e_lo[part, where] = halves(scaled)
        grad = product(y_hi[...], y_lo[...], e_hi[:, where], e_lo[:, where], ((1,), (0,)))
        for start in range(0, size, width):
            loss_sum[s : s + 1, :] += jnp.sum(loss[:, start : start + width], axis=0, keepdims=True)
        return grad

    def host_add(pair):
        where = lanes(pair, 2 * width)
        host_grad[...] += product(
            x_hi[0:padded, where], x_lo[0:padded, where], e_hi[:, where], e_lo[:, where], ((1,), (1,))
        )

    def host_add_odd(k):
        @pl.when(lax.rem(k, 2) == 1)
        def _():
            host_add(lax.div(k, 2))

    def update(vec, acc, k, grad):
        total = acc[k] + grad * grad
        acc[k] = total
        vec[k] = vec[k] - 0.05 * (grad * lax.rsqrt(total))

    pl.semaphore_wait(barrier, 9)
    each_chunk(lambda k: tile_copy(0, k).start())
    each_chunk(lambda k: tile_copy(1, k).start())
    x_hi[padded:kpad, :] = jnp.zeros((kpad - padded, words), BF16)
    x_lo[padded:kpad, :] = jnp.zeros((kpad - padded, words), BF16)
    for load in loads[:2]:
        load.wait()
    c_col[...] = turned(fill(c_vec, col_vec, col_cnt))
    each_chunk(lambda k: host_chunk(c_vec, k))
    for load in loads[2:6]:
        load.wait()
    r_logs = fill(r_vec, row_vec, row_cnt)
    fill_acc(r_acc, row_acc)
    loss_sum[...] = jnp.zeros_like(loss_sum)
    host_grad[...] = jnp.zeros_like(host_grad)

    def step0(k):
        prepare(0, k, c_col, True)
        grad = visit(0, r_vec[k], lanes(k))
        update(r_vec, r_acc, k, grad)
        out_copy(0, k).start()
        host_add_odd(k)

    each_chunk(step0)
    loads[6].wait()
    fill_acc(c_acc, col_acc)
    r_col[...] = turned(r_logs)

    def c_update(k):
        update(c_vec, c_acc, k, host_grad[:, lanes(k)])
        host_chunk(c_vec, k)

    each_chunk(c_update)
    host_grad[...] = jnp.zeros_like(host_grad)

    far = jnp.logical_or(lax.rem(r, 8) < 3, lax.rem(r, 2) == 0)

    @pl.when(jnp.logical_not(far))
    def _():
        each_chunk(lambda k: tile_copy(2, k).start())

    def visited(i, k):
        tile_copy(i, k).wait_recv()
        prepare(i + 1, k, c_col, True)
        out_copy(i, k).wait_recv()
        grad_out[i, k] = visit(i + 1, visitor_in[i, k], lanes(k))
        back_copy(i, k).start()
        host_add_odd(k)

    each_chunk(lambda k: visited(0, k))

    def c_sent(k):
        update(c_vec, c_acc, k, host_grad[:, lanes(k)])
        out_copy(1, k).start()

    each_chunk(c_sent)

    @pl.when(far)
    def _():
        each_chunk(lambda k: tile_copy(2, k).start())

    host_grad[...] = jnp.zeros_like(host_grad)

    each_chunk(lambda k: tile_copy(1, k).wait_recv())
    each_chunk(lambda k: prepare(2, k, r_col, False))

    def r_back(k):
        out_copy(0, k).wait_send()
        back_copy(0, k).wait_recv()
        update(r_vec, r_acc, k, grad_in[0, k])
        host_chunk(r_vec, k)

    each_chunk(r_back)

    def visited_pair(pair, carry):
        ks = [2 * pair, 2 * pair + 1]
        for k in ks:
            out_copy(1, k).wait_recv()
        x = jnp.concatenate([visitor_in[1, k] for k in ks], axis=1)
        grad = visit(2, x, lanes(pair, 2 * width))
        for j, k in enumerate(ks):
            grad_out[1, k] = grad[:, j * width : (j + 1) * width]
        grad_out[1, ks[1], depth + 1 : depth + 2, :] = loss_sum[2:3, :]
        for k in ks:
            back_copy(1, k).start()
        host_add(pair)
        return carry

    lax.fori_loop(0, nchunk // 2, visited_pair, 0)

    def r_sent(k):
        update(r_vec, r_acc, k, host_grad[:, lanes(k)])
        out_copy(2, k).start()

    each_chunk(r_sent)
    host_grad[...] = jnp.zeros_like(host_grad)

    def c_back(k):
        out_copy(1, k).wait_send()
        back_copy(1, k).wait_recv()
        update(c_vec, c_acc, k, grad_in[1, k])
        host_chunk(c_vec, k)

    each_chunk(c_back)
    each_chunk(lambda k: visited(2, k))

    outs = (out_row_vec, out_row_acc, out_col_vec, out_col_acc)

    def out_store(i, k):
        return pltpu.make_async_copy(
            out_stage.at[i, :, lanes(k)], outs[i].at[:, lanes(k)], store_sem.at[i, k]
        )

    def store(first, k, vec, acc):
        for i, ref in ((first, vec), (first + 1, acc)):
            out_stage[i, :, lanes(k)] = ref[k, 0:depth, :]
            out_store(i, k).start()

    def c_last(k):
        update(c_vec, c_acc, k, host_grad[:, lanes(k)])
        store(2, k, c_vec, c_acc)

    each_chunk(c_last)
    loss_sum[2:3, :] = grad_in[1, nchunk - 1, depth + 1 : depth + 2, :]
    for s in range(loss_sum.shape[0]):
        total = jnp.sum(loss_sum[s : s + 1, :], axis=1, keepdims=True)
        out_losses[0:1, s : s + 1] = total * (1.0 / (words * words))

    def r_last(k):
        out_copy(2, k).wait_send()
        back_copy(2, k).wait_recv()
        update(r_vec, r_acc, k, grad_in[2, k])
        store(0, k, r_vec, r_acc)

    each_chunk(r_last)

    def sent(k):
        for i in range(3):
            back_copy(i, k).wait_send()
            tile_copy(i, k).wait_send()
        for i in range(4):
            out_store(i, k).wait()

    each_chunk(sent)


def deliver(*refs):
    count = (len(refs) - 2) // 3
    sources, places, held = (refs[i * count : (i + 1) * count] for i in range(3))
    load_sem, store_sem = refs[-2:]
    loads, stores = [], []
    for source, place, stage in zip(sources, places, held):
        half = source.shape[1] // 2
        parts = (slice(0, half), slice(half, 2 * half)) if half % 128 == 0 else (slice(None),)
        for part in parts:
            i = len(loads)
            loads.append(pltpu.make_async_copy(source.at[:, part], stage.at[:, part], load_sem.at[i]))
            stores.append(pltpu.make_async_copy(stage.at[:, part], place.at[:, part], store_sem.at[i]))
    for load in loads:
        load.start()
    for load, store in zip(loads, stores):
        load.wait()
        store.start()
    for store in stores:
        store.wait()


def local(mesh, row_vec, row_acc, row_cnt, col_vec, col_acc, col_cnt, counts, log_total):
    depth, words = row_vec.shape
    nsteps = counts.shape[0]
    padded = -(-depth // 16) * 16
    kpad = -(-depth // 128) * 128
    nchunk = words // CHUNK
    chunks = (nchunk, padded, CHUNK)
    block = jax.ShapeDtypeStruct((depth, words), F32)
    vmem = pl.BlockSpec(memory_space=pltpu.VMEM)
    dma = pltpu.SemaphoreType.DMA
    hbm = pl.BlockSpec(memory_space=pltpu.HBM)
    results = (block,) * 4 + (jax.ShapeDtypeStruct((1, nsteps), F32),)
    trained = pl.pallas_call(
        functools.partial(kernel, depth, mesh.shape["row"], mesh.shape["col"]),
        out_shape=results,
        in_specs=[hbm] * 7 + [pl.BlockSpec(memory_space=pltpu.SMEM)],
        out_specs=(hbm,) * 4 + (vmem,),
        scratch_shapes=[
            pltpu.VMEM((4, depth, words), F32),
            pltpu.VMEM((depth, words), F32),
            pltpu.VMEM((depth, words), F32),
            pltpu.VMEM((1, words), jnp.int32),
            pltpu.VMEM((depth, words), F32),
            pltpu.VMEM((depth, words), F32),
            pltpu.VMEM((1, words), jnp.int32),
            pltpu.VMEM((nsteps, words, words), jnp.int32),
            pltpu.VMEM(chunks, F32),
            pltpu.VMEM(chunks, F32),
            pltpu.VMEM(chunks, F32),
            pltpu.VMEM(chunks, F32),
            pltpu.VMEM((3,) + chunks, F32),
            pltpu.VMEM((3,) + chunks, F32),
            pltpu.VMEM((3,) + chunks, F32),
            pltpu.VMEM((words, words), F32),
            pltpu.VMEM((words, words), F32),
            pltpu.VMEM((words, 128), F32),
            pltpu.VMEM((words, 128), F32),
            pltpu.VMEM((padded, words), BF16),
            pltpu.VMEM((padded, words), BF16),
            pltpu.VMEM((words, kpad), BF16),
            pltpu.VMEM((words, kpad), BF16),
            pltpu.VMEM((kpad, words), BF16),
            pltpu.VMEM((kpad, words), BF16),
            pltpu.VMEM((words, words), BF16),
            pltpu.VMEM((words, words), BF16),
            pltpu.VMEM((padded, words), F32),
            pltpu.VMEM((nsteps, CHUNK), F32),
            dma((7,)),
            dma((3, nchunk)),
            dma((3, nchunk)),
            dma((3, nchunk)),
            dma((3, nchunk)),
            dma((3, nchunk)),
            dma((3, nchunk)),
            dma((4, nchunk)),
        ],
        compiler_params=pltpu.CompilerParams(
            collective_id=0, has_side_effects=True, vmem_limit_bytes=62 * 1024 * 1024
        ),
        name="swivel",
    )(
        row_vec,
        row_acc,
        row_cnt.reshape(1, words),
        col_vec,
        col_acc,
        col_cnt.reshape(1, words),
        counts,
        log_total,
    )
    *arrays, losses = pl.pallas_call(
        deliver,
        out_shape=results,
        in_specs=[hbm] * 5,
        out_specs=(hbm,) * 5,
        scratch_shapes=[pltpu.VMEM(x.shape, x.dtype) for x in results] + [dma((9,)), dma((9,))],
        compiler_params=pltpu.CompilerParams(vmem_limit_bytes=62 * 1024 * 1024),
        name="deliver",
    )(*trained)
    return (*arrays, losses.T)


def solution(mesh):
    both = P(None, ("row", "col"))
    one = P(("row", "col"))
    return jax.shard_map(
        functools.partial(local, mesh),
        mesh=mesh,
        in_specs=(both, both, one, both, both, one, P(None, "row", "col"), P()),
        out_specs=(both,) * 5,
        check_vma=False,
    )
```

```python
import functools

import jax
import jax.numpy as jnp
from jax import lax
from jax.experimental import pallas as pl
from jax.experimental.pallas import tpu as pltpu
from jax.sharding import PartitionSpec as P

MESH = pl.DeviceIdType.MESH
F32 = jnp.float32
BF16 = jnp.bfloat16
CHUNK = 128
ROW_BLOCK = 128


def halves(x):
    hi = x.astype(BF16)
    return hi, (x - hi.astype(F32)).astype(BF16)


def product(a_hi, a_lo, b_hi, b_lo, dims):
    def dot(a, b):
        return lax.dot_general(a, b, (dims, ((), ())), preferred_element_type=F32)

    return dot(a_hi, b_hi) + (dot(a_hi, b_lo) + dot(a_lo, b_hi))


def kernel(
    depth,
    rows,
    cols,
    row_vec_hbm,
    row_acc_hbm,
    row_cnt_hbm,
    col_vec_hbm,
    col_acc_hbm,
    col_cnt_hbm,
    counts,
    log_total,
    out_row_vec,
    out_row_acc,
    out_col_vec,
    out_col_acc,
    out_losses,
    out_stage,
    row_vec,
    row_acc,
    row_cnt,
    col_vec,
    col_acc,
    col_cnt,
    tiles,
    r_vec,
    r_acc,
    c_vec,
    c_acc,
    visitor_in,
    grad_out,
    grad_in,
    base,
    conf,
    r_col,
    c_col,
    y_hi,
    y_lo,
    yt_hi,
    yt_lo,
    x_hi,
    x_lo,
    e_hi,
    e_lo,
    host_grad,
    loss_sum,
    local_sem,
    tile_send,
    tile_recv,
    out_send,
    out_recv,
    back_send,
    back_recv,
    store_sem,
):
    nchunk, padded, width = r_vec.shape
    words = row_vec.shape[1]
    kpad = x_hi.shape[0]
    r, c = lax.axis_index("row"), lax.axis_index("col")

    def at(dr, dc):
        return (lax.rem(r + dr + rows, rows), lax.rem(c + dc + cols, cols))

    def lanes(k, size=width):
        return pl.ds(pl.multiple_of(k * size, size), size)

    target = (at(-1, 1), at(2, -2), at(-3, 3))
    source = (at(1, -1), at(-2, 2), at(3, -3))
    tile_target = (at(-1, 0), at(0, -2), at(-3, 0))
    tile_source = (at(1, 0), at(0, 2), at(3, 0))

    barrier = pltpu.get_barrier_semaphore()
    for device in target + source + tile_source:
        pl.semaphore_signal(barrier, inc=1, device_id=device, device_id_type=MESH)

    loads = [
        pltpu.make_async_copy(src, dst, local_sem.at[i])
        for i, (src, dst) in enumerate(
            (
                (col_cnt_hbm, col_cnt),
                (col_vec_hbm, col_vec),
                (counts.at[0], tiles.at[0]),
                (row_cnt_hbm, row_cnt),
                (row_vec_hbm, row_vec),
                (row_acc_hbm, row_acc),
                (col_acc_hbm, col_acc),
            )
        )
    ]
    for load in loads:
        load.start()

    def tile_copy(i, k):
        rows_k = pl.ds(pl.multiple_of(k * width, width), width)
        return pltpu.make_async_remote_copy(
            src_ref=counts.at[i + 1, rows_k],
            dst_ref=tiles.at[i + 1, rows_k],
            send_sem=tile_send.at[i, k],
            recv_sem=tile_recv.at[i, k],
            device_id=tile_target[i],
            device_id_type=MESH,
        )

    def out_copy(i, k):
        return pltpu.make_async_remote_copy(
            src_ref=(c_vec if i == 1 else r_vec).at[k],
            dst_ref=visitor_in.at[i, k],
            send_sem=out_send.at[i, k],
            recv_sem=out_recv.at[i, k],
            device_id=target[i],
            device_id_type=MESH,
        )

    def back_copy(i, k):
        return pltpu.make_async_remote_copy(
            src_ref=grad_out.at[i, k],
            dst_ref=grad_in.at[i, k],
            send_sem=back_send.at[i, k],
            recv_sem=back_recv.at[i, k],
            device_id=source[i],
            device_id_type=MESH,
        )

    def each_chunk(body):
        def step(k, carry):
            body(k)
            return carry

        lax.fori_loop(0, nchunk, step, 0)

    logt = log_total[0]

    def real(x):
        return jnp.where(lax.broadcasted_iota(jnp.int32, x.shape, 0) < depth, x, 0.0)

    def fill(vec, vec_in, cnt):
        logs = jnp.log(cnt[...].astype(F32))
        for k in range(nchunk):
            part = slice(k * width, (k + 1) * width)
            vec[k, 0:depth, :] = vec_in[:, part]
            vec[k, depth : depth + 1, :] = logs[:, part]
            vec[k, depth + 1 : padded, :] = jnp.zeros((padded - depth - 1, width), F32)
        return logs

    def fill_acc(acc, acc_in):
        for k in range(nchunk):
            acc[k, 0:depth, :] = acc_in[:, k * width : (k + 1) * width]
            acc[k, depth:padded, :] = jnp.ones((padded - depth, width), F32)

    def turned(logs):
        return jnp.transpose(jnp.broadcast_to(logs, (128, words)))

    def host_chunk(vec, k):
        x = real(vec[k])
        y_hi[:, lanes(k)], y_lo[:, lanes(k)] = halves(x)
        xt = jnp.transpose(jnp.concatenate([x, jnp.zeros((kpad - padded, width), F32)], axis=0))
        yt_hi[lanes(k), :], yt_lo[lanes(k), :] = halves(xt)

    def prepare(i, k, column, turned):
        if turned:
            x = jnp.transpose(tiles[i, lanes(k), :].astype(F32))
        else:
            x = tiles[i, :, lanes(k)].astype(F32)
        q = jnp.log(jnp.maximum(x, 1.0))
        base[:, lanes(k)] = (q + logt) - column[:, 0:1]
        conf[:, lanes(k)] = jnp.where(x > 0, 0.1 + 0.25 * jnp.sqrt(x), 0.0)

    def visit(s, x, where):
        size = x.shape[1]
        words_log = x[depth : depth + 1, :]
        x_hi[0:padded, where], x_lo[0:padded, where] = halves(real(x))
        loss = jnp.zeros((8, size), F32)
        for start in range(0, words, ROW_BLOCK):
            part = slice(start, start + ROW_BLOCK)
            logits = product(
                yt_hi[part, :], yt_lo[part, :], x_hi[:, where], x_lo[:, where], ((1,), (0,))
            )
            weight = conf[part, where]
            err = logits - (base[part, where] - words_log)
            small = jnp.exp(-jnp.abs(err))
            positive = weight > 0
            scaled = jnp.where(
                positive, weight * err, jnp.where(err >= 0, 1.0, small) / (1.0 + small)
            )
            cell = jnp.where(
                positive, 0.5 * scaled * err, jnp.maximum(err, 0.0) + jnp.log1p(small)
            )
            loss = loss + jnp.sum(cell.reshape(ROW_BLOCK // 8, 8, size), axis=0)
            e_hi[part, where], e_lo[part, where] = halves(scaled)
        grad = product(y_hi[...], y_lo[...], e_hi[:, where], e_lo[:, where], ((1,), (0,)))
        for start in range(0, size, width):
            loss_sum[s : s + 1, :] += jnp.sum(loss[:, start : start + width], axis=0, keepdims=True)
        return grad

    def host_add(pair):
        where = lanes(pair, 2 * width)
        host_grad[...] += product(
            x_hi[0:padded, where], x_lo[0:padded, where], e_hi[:, where], e_lo[:, where], ((1,), (1,))
        )

    def host_add_odd(k):
        @pl.when(lax.rem(k, 2) == 1)
        def _():
            host_add(lax.div(k, 2))

    def update(vec, acc, k, grad):
        total = acc[k] + grad * grad
        acc[k] = total
        vec[k] = vec[k] - 0.05 * (grad * lax.rsqrt(total))

    pl.semaphore_wait(barrier, 9)
    each_chunk(lambda k: tile_copy(0, k).start())
    each_chunk(lambda k: tile_copy(1, k).start())
    x_hi[padded:kpad, :] = jnp.zeros((kpad - padded, words), BF16)
    x_lo[padded:kpad, :] = jnp.zeros((kpad - padded, words), BF16)
    for load in loads[:2]:
        load.wait()
    c_col[...] = turned(fill(c_vec, col_vec, col_cnt))
    each_chunk(lambda k: host_chunk(c_vec, k))
    for load in loads[2:6]:
        load.wait()
    r_logs = fill(r_vec, row_vec, row_cnt)
    fill_acc(r_acc, row_acc)
    loss_sum[...] = jnp.zeros_like(loss_sum)
    host_grad[...] = jnp.zeros_like(host_grad)

    def step0(k):
        prepare(0, k, c_col, True)
        grad = visit(0, r_vec[k], lanes(k))
        update(r_vec, r_acc, k, grad)
        out_copy(0, k).start()
        host_add_odd(k)

    each_chunk(step0)
    loads[6].wait()
    fill_acc(c_acc, col_acc)
    r_col[...] = turned(r_logs)

    def c_update(k):
        update(c_vec, c_acc, k, host_grad[:, lanes(k)])
        host_chunk(c_vec, k)

    each_chunk(c_update)
    host_grad[...] = jnp.zeros_like(host_grad)

    far = jnp.logical_or(lax.rem(r, 8) < 3, lax.rem(r, 2) == 0)

    @pl.when(jnp.logical_not(far))
    def _():
        each_chunk(lambda k: tile_copy(2, k).start())

    def visited(i, k):
        out_copy(i, k).wait_recv()
        grad_out[i, k] = visit(i + 1, visitor_in[i, k], lanes(k))
        back_copy(i, k).start()
        host_add_odd(k)

    def tile_in(i, k):
        tile_copy(i, k).wait_recv()
        prepare(i + 1, k, c_col, True)

    def step1(k):
        tile_in(0, k)
        visited(0, k)

    each_chunk(step1)

    def c_sent(k):
        update(c_vec, c_acc, k, host_grad[:, lanes(k)])
        out_copy(1, k).start()

    each_chunk(c_sent)

    @pl.when(far)
    def _():
        each_chunk(lambda k: tile_copy(2, k).start())

    host_grad[...] = jnp.zeros_like(host_grad)

    each_chunk(lambda k: tile_copy(1, k).wait_recv())
    each_chunk(lambda k: prepare(2, k, r_col, False))

    def r_back(k):
        out_copy(0, k).wait_send()
        back_copy(0, k).wait_recv()
        update(r_vec, r_acc, k, grad_in[0, k])
        host_chunk(r_vec, k)

    each_chunk(r_back)

    def visited_pair(pair, carry):
        ks = [2 * pair, 2 * pair + 1]
        for k in ks:
            out_copy(1, k).wait_recv()
        x = jnp.concatenate([visitor_in[1, k] for k in ks], axis=1)
        grad = visit(2, x, lanes(pair, 2 * width))
        for j, k in enumerate(ks):
            grad_out[1, k] = grad[:, j * width : (j + 1) * width]
        grad_out[1, ks[1], depth + 1 : depth + 2, :] = loss_sum[2:3, :]
        for k in ks:
            back_copy(1, k).start()
        host_add(pair)
        return carry

    lax.fori_loop(0, nchunk // 2, visited_pair, 0)

    def r_sent(k):
        update(r_vec, r_acc, k, host_grad[:, lanes(k)])
        out_copy(2, k).start()

    each_chunk(r_sent)
    host_grad[...] = jnp.zeros_like(host_grad)

    each_chunk(lambda k: tile_in(2, k))

    def c_back(k):
        out_copy(1, k).wait_send()
        back_copy(1, k).wait_recv()
        update(c_vec, c_acc, k, grad_in[1, k])
        host_chunk(c_vec, k)

    each_chunk(c_back)
    each_chunk(lambda k: visited(2, k))

    outs = (out_row_vec, out_row_acc, out_col_vec, out_col_acc)

    def out_store(i, k):
        return pltpu.make_async_copy(
            out_stage.at[i, :, lanes(k)], outs[i].at[:, lanes(k)], store_sem.at[i, k]
        )

    def store(first, k, vec, acc):
        for i, ref in ((first, vec), (first + 1, acc)):
            out_stage[i, :, lanes(k)] = ref[k, 0:depth, :]
            out_store(i, k).start()

    def c_last(k):
        update(c_vec, c_acc, k, host_grad[:, lanes(k)])
        store(2, k, c_vec, c_acc)

    each_chunk(c_last)
    loss_sum[2:3, :] = grad_in[1, nchunk - 1, depth + 1 : depth + 2, :]
    for s in range(loss_sum.shape[0]):
        total = jnp.sum(loss_sum[s : s + 1, :], axis=1, keepdims=True)
        out_losses[0:1, s : s + 1] = total * (1.0 / (words * words))

    def r_last(k):
        out_copy(2, k).wait_send()
        back_copy(2, k).wait_recv()
        update(r_vec, r_acc, k, grad_in[2, k])
        store(0, k, r_vec, r_acc)

    each_chunk(r_last)

    def sent(k):
        for i in range(3):
            back_copy(i, k).wait_send()
            tile_copy(i, k).wait_send()
        for i in range(4):
            out_store(i, k).wait()

    each_chunk(sent)


def deliver(*refs):
    count = (len(refs) - 2) // 3
    sources, places, held = (refs[i * count : (i + 1) * count] for i in range(3))
    load_sem, store_sem = refs[-2:]
    loads, stores = [], []
    for source, place, stage in zip(sources, places, held):
        half = source.shape[1] // 2
        parts = (slice(0, half), slice(half, 2 * half)) if half % 128 == 0 else (slice(None),)
        for part in parts:
            i = len(loads)
            loads.append(pltpu.make_async_copy(source.at[:, part], stage.at[:, part], load_sem.at[i]))
            stores.append(pltpu.make_async_copy(stage.at[:, part], place.at[:, part], store_sem.at[i]))
    for load in loads:
        load.start()
    for load, store in zip(loads, stores):
        load.wait()
        store.start()
    for store in stores:
        store.wait()


def local(mesh, row_vec, row_acc, row_cnt, col_vec, col_acc, col_cnt, counts, log_total):
    depth, words = row_vec.shape
    nsteps = counts.shape[0]
    padded = -(-depth // 16) * 16
    kpad = -(-depth // 128) * 128
    nchunk = words // CHUNK
    chunks = (nchunk, padded, CHUNK)
    block = jax.ShapeDtypeStruct((depth, words), F32)
    vmem = pl.BlockSpec(memory_space=pltpu.VMEM)
    dma = pltpu.SemaphoreType.DMA
    hbm = pl.BlockSpec(memory_space=pltpu.HBM)
    results = (block,) * 4 + (jax.ShapeDtypeStruct((1, nsteps), F32),)
    trained = pl.pallas_call(
        functools.partial(kernel, depth, mesh.shape["row"], mesh.shape["col"]),
        out_shape=results,
        in_specs=[hbm] * 7 + [pl.BlockSpec(memory_space=pltpu.SMEM)],
        out_specs=(hbm,) * 4 + (vmem,),
        scratch_shapes=[
            pltpu.VMEM((4, depth, words), F32),
            pltpu.VMEM((depth, words), F32),
            pltpu.VMEM((depth, words), F32),
            pltpu.VMEM((1, words), jnp.int32),
            pltpu.VMEM((depth, words), F32),
            pltpu.VMEM((depth, words), F32),
            pltpu.VMEM((1, words), jnp.int32),
            pltpu.VMEM((nsteps, words, words), jnp.int32),
            pltpu.VMEM(chunks, F32),
            pltpu.VMEM(chunks, F32),
            pltpu.VMEM(chunks, F32),
            pltpu.VMEM(chunks, F32),
            pltpu.VMEM((3,) + chunks, F32),
            pltpu.VMEM((3,) + chunks, F32),
            pltpu.VMEM((3,) + chunks, F32),
            pltpu.VMEM((words, words), F32),
            pltpu.VMEM((words, words), F32),
            pltpu.VMEM((words, 128), F32),
            pltpu.VMEM((words, 128), F32),
            pltpu.VMEM((padded, words), BF16),
            pltpu.VMEM((padded, words), BF16),
            pltpu.VMEM((words, kpad), BF16),
            pltpu.VMEM((words, kpad), BF16),
            pltpu.VMEM((kpad, words), BF16),
            pltpu.VMEM((kpad, words), BF16),
            pltpu.VMEM((words, words), BF16),
            pltpu.VMEM((words, words), BF16),
            pltpu.VMEM((padded, words), F32),
            pltpu.VMEM((nsteps, CHUNK), F32),
            dma((7,)),
            dma((3, nchunk)),
            dma((3, nchunk)),
            dma((3, nchunk)),
            dma((3, nchunk)),
            dma((3, nchunk)),
            dma((3, nchunk)),
            dma((4, nchunk)),
        ],
        compiler_params=pltpu.CompilerParams(
            collective_id=0, has_side_effects=True, vmem_limit_bytes=62 * 1024 * 1024
        ),
        name="swivel",
    )(
        row_vec,
        row_acc,
        row_cnt.reshape(1, words),
        col_vec,
        col_acc,
        col_cnt.reshape(1, words),
        counts,
        log_total,
    )
    *arrays, losses = pl.pallas_call(
        deliver,
        out_shape=results,
        in_specs=[hbm] * 5,
        out_specs=(hbm,) * 5,
        scratch_shapes=[pltpu.VMEM(x.shape, x.dtype) for x in results] + [dma((9,)), dma((9,))],
        compiler_params=pltpu.CompilerParams(vmem_limit_bytes=62 * 1024 * 1024),
        name="deliver",
    )(*trained)
    return (*arrays, losses.T)


def solution(mesh):
    both = P(None, ("row", "col"))
    one = P(("row", "col"))
    return jax.shard_map(
        functools.partial(local, mesh),
        mesh=mesh,
        in_specs=(both, both, one, both, both, one, P(None, "row", "col"), P()),
        out_specs=(both,) * 5,
        check_vma=False,
    )
```
